32 devices in a mesh: sub: 8 (over z, y), ifc: 4 (over x, core).
Axes of the slice: x: 2, y: 2, z: 4, core: 2. Of those that a mesh axis runs over, the one named last changes fastest.
Arguments:
- gap: float32 [8, 1024, 128], P('sub', 'ifc'), may hold values from -6 to 6
- flexibility: float32 [8, 2, 1024, 2048], P('sub', None, 'ifc'), may hold values from -1 to 4, as said below
- stiffness: float32 [8, 2, 1024, 2048], P('sub', None, 'ifc'), may hold values from -1 to 4, as said below
- modes: float32 [8, 6, 2, 1024], P('sub', None, None, 'ifc'), may hold values from -1 to 1
- mode_counts: int32 [8], P('sub'), may hold values from 3 to 6
Outputs:
- multipliers: float32 [8, 1024, 128], P('sub', 'ifc')
- residual: float32 [8, 1024, 128], P('sub', 'ifc')
The draws below stay inside these ranges and needn't reach their ends.
Inputs may be any that keep to these rules, and one draw needn't show every extreme that they name: `flexibility`: each subdomain's block, as a matrix of order 2 * 1024, is symmetric positive definite. `stiffness`: each subdomain's block, as a matrix of order 2 * 1024, is symmetric positive definite.
All inputs are finite; a program needn't handle non-finite values.
Results may differ from the reference program's by a relative error of at most 0.0003.
Values sent between devices are 32-bit elements; how exact they have to be, the bound alone decides.
A program may use at most 64 MiB of HBM per device.

```python
import math
import jax
import jax.numpy as jnp
from jax import lax

FACE = 1024
MODES = 6
LOADS = 128
ITERS = 1
SUBS = 8


def spd_block(key):
    order = 2 * FACE
    key_off, key_diag = jax.random.split(key)
    bound_off = 0.5 / math.sqrt(order)
    offdiag = jax.random.uniform(key_off, (SUBS, order, order), jnp.float32, -bound_off, bound_off)
    diagonal = jax.random.uniform(key_diag, (SUBS, order), jnp.float32, 1.0, 2.0)
    symmetric = (offdiag + jnp.swapaxes(offdiag, 1, 2)) * 0.5
    matrix = symmetric + jnp.eye(order, dtype=jnp.float32)[None] * diagonal[:, :, None]
    return matrix.reshape(SUBS, 2, FACE, 2 * FACE)


def draw_flexibility(key, part):
    return spd_block(jax.random.fold_in(key, 101))


def draw_stiffness(key, part):
    return spd_block(jax.random.fold_in(key, 202))


def draw_modes(key, part):
    key_base, key_right, key_left = jax.random.split(jax.random.fold_in(key, 303), 3)
    shape = (SUBS, MODES, FACE)
    base = jnp.clip(jax.random.normal(key_base, shape, jnp.float32), -5.0, 5.0)
    right_noise = jnp.clip(jax.random.normal(key_right, shape, jnp.float32), -5.0, 5.0)
    left_noise = jnp.clip(jax.random.normal(key_left, shape, jnp.float32), -5.0, 5.0)
    right_face = base + 0.1 * right_noise
    left_face = jnp.roll(base, 1, axis=0) + 0.1 * left_noise
    scale = 1.0 / math.sqrt(2.0 * FACE)
    return jnp.stack([left_face, right_face], 2) * scale


def set_ends(entries, key, least, largest):
    dims = entries.shape
    index_at = [jax.random.randint(jax.random.fold_in(key, axis), (), 0, dims[axis]) for axis in range(len(dims))]
    entries = entries.at[tuple(index_at)].set(least)
    longest = dims.index(max(dims))
    index_at[longest] = (index_at[longest] + 1) % dims[longest]
    return entries.at[tuple(index_at)].set(largest)


def block_levels(own_key, extent, cuts, low, high):
    gain, own = 1.0, jax.random.fold_in(own_key, 6)
    for axis_at, parts in cuts:
        heights = jnp.exp(jax.random.uniform(jax.random.fold_in(own, axis_at), (parts,), jnp.float32, low / len(cuts), high / len(cuts)))
        gain = gain * jnp.repeat(heights, extent[axis_at] // parts).reshape([-1 if axis == axis_at else 1 for axis in range(len(extent))])
    return gain


def bell_draw(rng, shape, width, reach, pieces=(), kind=jnp.bfloat16):
    entries = width * jax.random.normal(rng, shape, jnp.float32)
    if pieces:
        entries = entries * block_levels(rng, shape, pieces, -0.22, 0.18)
    return jnp.clip(entries, -reach, reach).astype(kind)


def setup_inputs(seed: int = 0) -> dict:
    key_of = jax.random.split(jax.random.key(seed), 6)
    return {
        "gap": bell_draw(key_of[0], (SUBS, FACE, LOADS), 1.0, 6.0, ((0, 8), (1, 4)), jnp.float32),
        "flexibility": draw_flexibility(jax.random.fold_in(key_of[5], 71), 0),
        "stiffness": draw_stiffness(jax.random.fold_in(key_of[5], 71), 0),
        "modes": draw_modes(jax.random.fold_in(key_of[5], 71), 0),
        "mode_counts": set_ends(jax.random.randint(key_of[4], (SUBS,), 3, 7), jax.random.fold_in(key_of[4], 1), 3, 6).astype(jnp.int32),
    }


precise = lax.Precision.HIGHEST

def assemble(own_blocks, next_blocks, off_blocks):
    subs_count = own_blocks.shape[0]
    mode_count = own_blocks.shape[1]
    shifted = jnp.concatenate([jnp.zeros((1, mode_count, mode_count), jnp.float32), next_blocks[:-1]], 0)
    diag_blocks = own_blocks + shifted
    ident = jnp.eye(subs_count, dtype=jnp.float32)
    upper = jnp.eye(subs_count, k=1, dtype=jnp.float32)
    whole = jnp.einsum('st,sij->sitj', ident, diag_blocks, precision=precise)
    whole = whole + jnp.einsum('st,sij->sitj', upper, off_blocks, precision=precise)
    whole = whole + jnp.einsum('st,sij->tjsi', upper, off_blocks, precision=precise)
    return whole.reshape(subs_count * mode_count, subs_count * mode_count)

def coarse_solve(factor, rhs_matrix):
    forward = lax.linalg.triangular_solve(factor, rhs_matrix, left_side=True, lower=True)
    return lax.linalg.triangular_solve(factor, forward, left_side=True, lower=True, transpose_a=True)

def reference(gap, flexibility, stiffness, modes, mode_counts):
    edge_live = (jnp.arange(SUBS) < SUBS - 1).astype(jnp.float32)[:, None, None]
    active = (jnp.arange(MODES)[None, :] < mode_counts[:, None]).astype(jnp.float32)
    mode_right = modes[:, :, 1] * active[:, :, None] * edge_live
    mode_left = modes[:, :, 0] * active[:, :, None]
    mode_next = jnp.concatenate([mode_left[1:], jnp.zeros((1, MODES, FACE), jnp.float32)], 0)
    own_blocks = jnp.einsum('smi,sni->smn', mode_right, mode_right, precision=precise)
    own_blocks = own_blocks + jnp.eye(MODES, dtype=jnp.float32)[None] * (1.0 - active)[:, :, None]
    next_blocks = jnp.einsum('smi,sni->smn', mode_next, mode_next, precision=precise)
    off_blocks = -jnp.einsum('smi,sni->smn', mode_right, mode_next, precision=precise)
    factor = jnp.linalg.cholesky(assemble(own_blocks, next_blocks, off_blocks))

    def project(vector):
        own_part = jnp.einsum('smi,sik->smk', mode_right, vector, precision=precise)
        next_part = -jnp.einsum('smi,sik->smk', mode_next, vector, precision=precise)
        coarse_rhs = own_part + jnp.concatenate([jnp.zeros((1, MODES, LOADS), jnp.float32), next_part[:-1]], 0)
        weights = coarse_solve(factor, coarse_rhs.reshape(SUBS * MODES, LOADS)).reshape(SUBS, MODES, LOADS)
        later = jnp.concatenate([weights[1:], jnp.zeros((1, MODES, LOADS), jnp.float32)], 0)
        correction = jnp.einsum('smi,smk->sik', mode_right, weights, precision=precise)
        correction = correction - jnp.einsum('smi,smk->sik', mode_next, later, precision=precise)
        return vector - correction

    def apply_jump(matrix, vector):
        before = jnp.concatenate([jnp.zeros((1, FACE, LOADS), jnp.float32), vector[:-1]], 0)
        traces = jnp.stack([-before, vector], 1).reshape(SUBS, 2 * FACE, LOADS)
        image = jnp.einsum('sim,smk->sik', matrix.reshape(SUBS, 2 * FACE, 2 * FACE), traces, precision=precise)
        image = image.reshape(SUBS, 2, FACE, LOADS)
        after = jnp.concatenate([image[1:, 0], jnp.zeros((1, FACE, LOADS), jnp.float32)], 0)
        return (image[:, 1] - after) * edge_live

    def inner(first_vec, second_vec):
        return jnp.sum(first_vec * second_vec, axis=(0, 1))

    def precond(vector):
        return project(0.25 * apply_jump(stiffness, vector))
    multipliers = jnp.zeros((SUBS, FACE, LOADS), jnp.float32)
    residual = project(gap * edge_live)
    search = precond(residual)
    direction = search
    rz_now = inner(residual, search)
    for iteration in range(ITERS):
        image = project(apply_jump(flexibility, direction))
        step_size = rz_now / inner(direction, image)
        multipliers = multipliers + step_size * direction
        residual = residual - step_size * image
        if iteration + 1 < ITERS:
            search = precond(residual)
            rz_new = inner(residual, search)
            direction = search + rz_new / rz_now * direction
            rz_now = rz_new
    return (multipliers, residual)
```

```python
import functools

import jax
import jax.numpy as jnp
from jax import lax
from jax.experimental import pallas as pl
from jax.experimental.pallas import tpu as pltpu
from jax.sharding import PartitionSpec as P

MESH = pl.DeviceIdType.MESH
precise = lax.Precision.HIGHEST
f32 = jnp.float32


def dot_nn(a, b):
    return lax.dot_general(a, b, (((1,), (0,)), ((), ())), precision=precise, preferred_element_type=f32)


def dot_nt(a, b):
    return lax.dot_general(a, b, (((1,), (1,)), ((), ())), precision=precise, preferred_element_type=f32)


def dot_tn(a, b):
    return lax.dot_general(a, b, (((0,), (0,)), ((), ())), precision=precise, preferred_element_type=f32)


def split(a):
    hi = a.astype(jnp.bfloat16)
    lo = (a - hi.astype(f32)).astype(jnp.bfloat16)
    return hi, lo


def kernel(S, L, R, gap_ref, k_hbm, f_hbm, modes_ref, mult_ref, res_ref,
           k_v, f_v, nbm, mt, t_buf, nbg, u_buf, nbu, v_buf, nbv, part, red, wbuf, own, acc,
           load_sem, nb_send, nb_recv, ag_send, ag_recv, mt_send, mt_recv,
           ln_send, ln_recv, sb_send, sb_recv):
    X = L // 2
    n = 8 * S
    nw = -(-n // 128) * 128
    s = lax.axis_index("sub")
    lane = lax.axis_index("ifc")
    x, core = lane // 2, lane % 2
    mate = x * 2 + (1 - core)
    has_l, has_r = s > 0, s < S - 1
    m_l, m_r = has_l.astype(f32), has_r.astype(f32)
    left, right = jnp.maximum(s - 1, 0), jnp.minimum(s + 1, S - 1)

    loads = [pltpu.make_async_copy(k_hbm, k_v, load_sem.at[0]),
             pltpu.make_async_copy(f_hbm, f_v, load_sem.at[1])]
    for load in loads:
        load.start()

    def rc(src, dst, ss, rs, sub, ln):
        return pltpu.make_async_remote_copy(src_ref=src, dst_ref=dst, send_sem=ss, recv_sem=rs,
                                            device_id=(sub, ln), device_id_type=MESH)

    barrier = pltpu.get_barrier_semaphore()
    for d in range(1, L):
        pl.semaphore_signal(barrier, inc=1, device_id=(s, lax.rem(lane + d, L)), device_id_type=MESH)
    for d in range(1, S):
        pl.semaphore_signal(barrier, inc=1, device_id=(lax.rem(s + d, S), lane), device_id_type=MESH)

    t_buf[0, 1, lane] = gap_ref[...] * m_r

    @pl.when(jnp.logical_not(has_l))
    def _():
        nbm[0] = jnp.zeros_like(nbm[0])
        nbg[...] = jnp.zeros_like(nbg)
        nbu[0] = jnp.zeros_like(nbu[0])

    @pl.when(jnp.logical_not(has_r))
    def _():
        nbm[1] = jnp.zeros_like(nbm[1])
        nbu[1] = jnp.zeros_like(nbu[1])
        nbv[...] = jnp.zeros_like(nbv)

    pl.semaphore_wait(barrier, (L - 1) + (S - 1))

    to_left = {
        0: rc(modes_ref.at[pl.ds(0, 16)], nbm.at[1], nb_send.at[0], nb_recv.at[0], left, lane),
        3: rc(u_buf.at[0], nbu.at[1], nb_send.at[3], nb_recv.at[3], left, lane),
        5: rc(v_buf, nbv, nb_send.at[5], nb_recv.at[5], left, lane),
    }
    to_right = {
        1: rc(modes_ref.at[pl.ds(0, 16)], nbm.at[0], nb_send.at[1], nb_recv.at[1], right, lane),
        2: rc(t_buf.at[0, 1, lane], nbg, nb_send.at[2], nb_recv.at[2], right, lane),
        4: rc(u_buf.at[1], nbu.at[0], nb_send.at[4], nb_recv.at[4], right, lane),
    }

    def nb_start(which):
        copy, cond = (to_left[which], has_l) if which in to_left else (to_right[which], has_r)

        @pl.when(cond)
        def _():
            copy.start()

    def nb_wait(which):
        copy, cond = (to_left[which], has_r) if which in to_left else (to_right[which], has_l)

        @pl.when(cond)
        def _():
            copy.wait_recv()

    sends = []

    def ag_copy(r, f, src, slot, dst):
        piece = t_buf.at[r, f, src]
        return rc(piece, piece, ag_send.at[r, f, slot], ag_recv.at[r, f, src], s, dst)

    def ag_start(r, f):
        for d in range(1, X):
            copy = ag_copy(r, f, lane, d, lax.rem(x + d, X) * 2 + core)
            copy.start()
            sends.append(copy)
        copy = ag_copy(r, f, lane, 0, mate)
        copy.start()
        sends.append(copy)

    def ag_forward(r, f):
        for d in range(1, X):
            src = lax.rem(x + d, X) * 2 + core
            copy = ag_copy(r, f, src, X - 1 + d, mate)
            copy.wait_recv()
            copy.start()
            sends.append(copy)

    def lane_send(r, rows):
        for d in range(1, L):
            block = part.at[r, lane, pl.ds(0, rows)]
            copy = rc(block, block, ln_send.at[r, d], ln_recv.at[r, lane], s, lax.rem(lane + d, L))
            copy.start()
            sends.append(copy)

    def lane_sum(r, rows):
        total = part[r, lane, 0:rows]
        for d in range(1, L):
            src = lax.rem(lane + d, L)
            block = part.at[r, src, pl.ds(0, rows)]
            rc(block, block, ln_send.at[r, d], ln_recv.at[r, src], s, src).wait_recv()
            total = total + part[r, src, 0:rows]
        return total

    def sub_send(r, rows, value):
        red[r, s, 0:rows] = value
        block = red.at[r, s, pl.ds(0, rows)]
        for d in range(1, S):
            copy = rc(block, block, sb_send.at[r, d], sb_recv.at[r, s], lax.rem(s + d, S), lane)
            copy.start()
            sends.append(copy)

    def sub_wait(r, rows):
        for d in range(1, S):
            src = lax.rem(s + d, S)
            block = red.at[r, src, pl.ds(0, rows)]
            rc(block, block, sb_send.at[r, d], sb_recv.at[r, src], src, lane).wait_recv()

    def rhs_of(r):
        rows = []
        for t in range(S):
            row = red[r, t, 8:16]
            if t > 0:
                row = row + red[r, t - 1, 16:24]
            if t < S - 1:
                row = row + red[r, t + 1, 0:8]
            rows.append(row)
        return jnp.concatenate(rows, 0)

    def inner_of(r):
        total = red[r, 0, 24:25]
        for t in range(1, S):
            total = total + red[r, t, 24:25]
        return total

    def weights_of(r, inverse):
        wbuf[r, 0:8] = jnp.zeros((8, 128), f32)
        wbuf[r, n + 8:n + 16] = jnp.zeros((8, 128), f32)
        wbuf[r, 8:n + 8] = dot_nn(inverse, rhs_of(r))
        return wbuf[r, pl.ds(pl.multiple_of(s * 8, 8), 24)]

    nb_start(0)
    nb_start(1)
    ag_start(0, 1)
    nb_start(2)
    nb_wait(0)
    nb_wait(1)
    modes_left, modes_right = modes_ref[0:8], modes_ref[8:16]
    zero = jnp.zeros((8, R), f32)
    mt_l = jnp.concatenate([-nbm[0, 8:16], modes_left * m_l, zero], 0)
    mt_r = jnp.concatenate([zero, modes_right, -nbm[1, 0:8]], 0)
    mt[lane, 0] = mt_l
    mt[lane, 1] = mt_r
    gram = dot_nt(mt_l[8:16], mt_l) + dot_nt(mt_r[8:16], mt_r)
    part[0, lane, 0:24] = dot_nn(mt_r, t_buf[0, 1, lane])
    part[0, lane, 24:32] = jnp.concatenate([gram, jnp.zeros((8, 104), f32)], 1)
    lane_send(0, 32)
    for d in range(1, L):
        copy = rc(mt.at[lane], mt.at[lane], mt_send.at[d], mt_recv.at[lane], s, lax.rem(lane + d, L))
        copy.start()
        sends.append(copy)
    nb_wait(2)
    t_buf[0, 0, lane] = -nbg[...]
    ag_start(0, 0)
    total = lane_sum(0, 32)
    idle = jnp.where(
        lax.broadcasted_iota(jnp.int32, (8, 128), 0) + 8 == lax.broadcasted_iota(jnp.int32, (8, 128), 1),
        modes_ref[16:24, 0:128], 0.0)
    sub_send(0, 32, jnp.concatenate([total[0:24], total[24:32] + idle], 0))
    ag_forward(0, 1)
    sub_wait(0, 32)

    rows = []
    for t in range(S):
        row = red[0, t, 24:32]
        if nw > 128:
            row = jnp.concatenate([row, jnp.zeros((8, nw - 128), f32)], 1)
        rows.append(pltpu.roll(row, (8 * (t - 1)) % nw, 1) if t != 1 else row)
    coarse = jnp.concatenate(rows, 0)
    row_at = lax.broadcasted_iota(jnp.int32, (n, nw), 0)
    col_at = lax.broadcasted_iota(jnp.int32, (n, nw), 1)

    def sweep(a, k, row):
        col = jnp.sum(jnp.where(col_at == k, a, 0.0), axis=1, keepdims=True)
        pivot = jnp.sum(jnp.where(col_at[0:1] == k, row, 0.0), axis=1, keepdims=True)
        scale = 1.0 / pivot
        scaled = jnp.where(col_at[0:1] == k, -scale, row * scale)
        base = jnp.where(col_at == k, 0.0, a)
        col = jnp.where(row_at[:, 0:1] == k, -1.0, col)
        return jnp.where(row_at == k, scaled, base - col * jnp.where(col_at[0:1] == k, -scale, row * scale))

    if n <= 64:
        for t in range(S):
            for m in range(6):
                k = 8 * t + m
                coarse = sweep(coarse, k, coarse[k:k + 1])
    else:
        def step(i, a):
            k = 8 * (i // 6) + lax.rem(i, 6)
            return sweep(a, k, jnp.sum(jnp.where(row_at == k, a, 0.0), axis=0, keepdims=True))
        coarse = lax.fori_loop(0, 6 * S, step, coarse)
    pad = lax.rem(row_at, 8) >= 6
    inverse = jnp.where(pad, jnp.where(row_at == col_at, 1.0, 0.0), -coarse)[:, 0:n]

    ag_forward(0, 0)
    for d in range(1, L):
        src = lax.rem(lane + d, L)
        rc(mt.at[src], mt.at[src], mt_send.at[d], mt_recv.at[src], s, src).wait_recv()

    def multiply(r, matrix, weights):
        acc[...] = jnp.zeros_like(acc)
        order = [(lane, False), (mate, True)]
        order += [(lax.rem(x + d, X) * 2 + core, False) for d in range(1, X)]
        order += [(lax.rem(x + d, X) * 2 + 1 - core, True) for d in range(1, X)]
        for j, wait in order:
            for f in (1, 0):
                if wait:
                    ag_copy(r, f, j, 0, mate).wait_recv()
                piece = t_buf[r, f, j] - dot_tn(mt[j, f], weights)
                if j is lane:
                    own[r, f] = piece
                columns = pl.ds(pl.multiple_of(f * (L * R) + j * R, R), R)
                p_hi, p_lo = split(piece)
                for h in range(2):
                    m_hi, m_lo = split(matrix[h, :, columns])
                    acc[h] += (
                        jnp.dot(m_hi, p_hi, preferred_element_type=f32)
                        + jnp.dot(m_hi, p_lo, preferred_element_type=f32)
                        + jnp.dot(m_lo, p_hi, preferred_element_type=f32)
                    )

    weights = weights_of(0, inverse)
    loads[0].wait()
    multiply(0, k_v, weights)

    u_buf[0] = acc[0] * 0.25
    u_buf[1] = acc[1] * 0.25
    nb_start(3)
    nb_start(4)
    dots = jnp.sum(own[0, 0] * u_buf[0] + own[0, 1] * u_buf[1], axis=0, keepdims=True)
    part[1, lane, 0:24] = dot_nn(mt_l, u_buf[0]) + dot_nn(mt_r, u_buf[1])
    part[1, lane, 24:32] = jnp.broadcast_to(dots, (8, 128))
    lane_send(1, 32)
    nb_wait(3)
    t_buf[1, 1, lane] = (u_buf[1] - nbu[1]) * m_r
    ag_start(1, 1)
    nb_wait(4)
    t_buf[1, 0, lane] = (u_buf[0] - nbu[0]) * m_l
    ag_start(1, 0)
    sub_send(1, 32, lane_sum(1, 32))
    ag_forward(1, 1)
    ag_forward(1, 0)
    sub_wait(1, 32)
    weights = weights_of(1, inverse)
    loads[1].wait()
    multiply(1, f_v, weights)

    v_buf[...] = acc[0]
    nb_start(5)
    dots = jnp.sum(own[1, 0] * acc[0] + own[1, 1] * acc[1], axis=0, keepdims=True)
    part[2, lane, 0:24] = dot_nn(mt_l, acc[0]) + dot_nn(mt_r, acc[1])
    part[2, lane, 24:32] = jnp.broadcast_to(dots, (8, 128))
    lane_send(2, 32)
    sub_send(2, 32, lane_sum(2, 32))
    nb_wait(5)
    image = (acc[1] - nbv[...]) * m_r
    sub_wait(2, 32)
    step_size = inner_of(1) / inner_of(2)
    image = image - dot_tn(mt_r, weights_of(2, inverse))
    mult_ref[...] = step_size * own[1, 1]
    res_ref[...] = own[0, 1] - step_size * image

    for copy in sends:
        copy.wait_send()

    @pl.when(has_l)
    def _():
        for copy in to_left.values():
            copy.wait_send()

    @pl.when(has_r)
    def _():
        for copy in to_right.values():
            copy.wait_send()


def per_device(gap, flexibility, stiffness, modes, mode_counts):
    S, L = lax.axis_size("sub"), lax.axis_size("ifc")
    R, n = gap.shape[1], 8 * lax.axis_size("sub")
    count, loads = modes.shape[1], gap.shape[2]
    live = (lax.axis_index("sub") < S - 1).astype(f32)
    active = (jnp.arange(8) < mode_counts[0]).astype(f32)
    faces = jnp.pad(jnp.swapaxes(modes[0], 0, 1), ((0, 0), (0, 8 - count), (0, 0)))
    faces = faces * active[None, :, None]
    idle = jnp.broadcast_to(1.0 - active[:, None], (8, R))
    packed = jnp.concatenate([faces[0], faces[1] * live, idle], 0)
    vm = pl.BlockSpec(memory_space=pltpu.VMEM)
    hbm = pl.BlockSpec(memory_space=pl.ANY)
    dma = pltpu.SemaphoreType.DMA
    mult, res = pl.pallas_call(
        functools.partial(kernel, S, L, R),
        out_shape=[jax.ShapeDtypeStruct((R, loads), f32)] * 2,
        in_specs=[vm, hbm, hbm, vm],
        out_specs=[vm, vm],
        scratch_shapes=[
            pltpu.VMEM((2, R, 2 * L * R), f32),
            pltpu.VMEM((2, R, 2 * L * R), f32),
            pltpu.VMEM((2, 16, R), f32),
            pltpu.VMEM((L, 2, 24, R), f32),
            pltpu.VMEM((2, 2, L, R, loads), f32),
            pltpu.VMEM((R, loads), f32),
            pltpu.VMEM((2, R, loads), f32),
            pltpu.VMEM((2, R, loads), f32),
            pltpu.VMEM((R, loads), f32),
            pltpu.VMEM((R, loads), f32),
            pltpu.VMEM((3, L, 32, 128), f32),
            pltpu.VMEM((3, S, 32, 128), f32),
            pltpu.VMEM((3, n + 16, 128), f32),
            pltpu.VMEM((2, 2, R, loads), f32),
            pltpu.VMEM((2, R, loads), f32),
            dma((2,)),
            dma((6,)),
            dma((6,)),
            dma((2, 2, L)),
            dma((2, 2, L)),
            dma((L,)),
            dma((L,)),
            dma((3, L)),
            dma((3, L)),
            dma((3, S)),
            dma((3, S)),
        ],
        compiler_params=pltpu.CompilerParams(
            collective_id=0, has_side_effects=True, vmem_limit_bytes=48 * 1024 * 1024
        ),
    )(gap[0], stiffness[0], flexibility[0], packed)
    return (mult[None], res[None])


def solution(mesh):
    return jax.shard_map(
        per_device,
        mesh=mesh,
        in_specs=(
            P("sub", "ifc", None),
            P("sub", None, "ifc", None),
            P("sub", None, "ifc", None),
            P("sub", None, None, "ifc"),
            P("sub"),
        ),
        out_specs=(P("sub", "ifc", None), P("sub", "ifc", None)),
        check_vma=False,
    )
```

```python
import functools

import jax
import jax.numpy as jnp
from jax import lax
from jax.experimental import pallas as pl
from jax.experimental.pallas import tpu as pltpu
from jax.sharding import PartitionSpec as P

MESH = pl.DeviceIdType.MESH
precise = lax.Precision.HIGHEST
f32 = jnp.float32


def dot_nn(a, b):
    return lax.dot_general(a, b, (((1,), (0,)), ((), ())), precision=precise, preferred_element_type=f32)


def dot_nt(a, b):
    return lax.dot_general(a, b, (((1,), (1,)), ((), ())), precision=precise, preferred_element_type=f32)


def dot_tn(a, b):
    return lax.dot_general(a, b, (((0,), (0,)), ((), ())), precision=precise, preferred_element_type=f32)


def split(a):
    hi = a.astype(jnp.bfloat16)
    lo = (a - hi.astype(f32)).astype(jnp.bfloat16)
    return hi, lo


def thirds(a):
    hi = a.astype(jnp.bfloat16).astype(f32)
    mid = (a - hi).astype(jnp.bfloat16).astype(f32)
    lo = (a - hi - mid).astype(jnp.bfloat16).astype(f32)
    return hi, mid, lo


def rows_times(a, b):
    count, width = a.shape[0], b.shape[1]
    hi = a.astype(jnp.bfloat16).astype(f32)
    tall = jnp.concatenate([hi, a - hi], 0).astype(jnp.bfloat16)
    wide = jnp.dot(tall, jnp.concatenate(split(b), 1), preferred_element_type=f32)
    wide = wide[:count] + wide[count:]
    return wide[:, :width] + wide[:, width:]


def kernel(S, L, R, gap_ref, k_hbm, f_hbm, modes_ref, mult_ref, res_ref,
           k_v, f_v, nbm, mt, t_buf, nbg, u_buf, nbu, v_buf, nbv, part, red, wbuf, own, acc, mt_t, acc2,
           load_sem, nb_send, nb_recv, ag_send, ag_recv, mt_send, mt_recv,
           ln_send, ln_recv, sb_send, sb_recv):
    X = L // 2
    n = 8 * S
    nw = -(-n // 128) * 128
    s = lax.axis_index("sub")
    lane = lax.axis_index("ifc")
    x, core = lane // 2, lane % 2
    mate = x * 2 + (1 - core)
    has_l, has_r = s > 0, s < S - 1
    m_l, m_r = has_l.astype(f32), has_r.astype(f32)
    left, right = jnp.maximum(s - 1, 0), jnp.minimum(s + 1, S - 1)

    loads = [pltpu.make_async_copy(k_hbm, k_v, load_sem.at[0]),
             pltpu.make_async_copy(f_hbm, f_v, load_sem.at[1])]
    for load in loads:
        load.start()

    def rc(src, dst, ss, rs, sub, ln):
        return pltpu.make_async_remote_copy(src_ref=src, dst_ref=dst, send_sem=ss, recv_sem=rs,
                                            device_id=(sub, ln), device_id_type=MESH)

    barrier = pltpu.get_barrier_semaphore()
    for d in range(1, L):
        pl.semaphore_signal(barrier, inc=1, device_id=(s, lax.rem(lane + d, L)), device_id_type=MESH)
    for d in range(1, S):
        pl.semaphore_signal(barrier, inc=1, device_id=(lax.rem(s + d, S), lane), device_id_type=MESH)

    t_buf[0, 1, lane] = gap_ref[...] * m_r

    @pl.when(jnp.logical_not(has_l))
    def _():
        nbm[0] = jnp.zeros_like(nbm[0])
        nbg[...] = jnp.zeros_like(nbg)
        nbu[0] = jnp.zeros_like(nbu[0])

    @pl.when(jnp.logical_not(has_r))
    def _():
        nbm[1] = jnp.zeros_like(nbm[1])
        nbu[1] = jnp.zeros_like(nbu[1])
        nbv[...] = jnp.zeros_like(nbv)

    pl.semaphore_wait(barrier, (L - 1) + (S - 1))

    to_left = {
        0: rc(modes_ref.at[pl.ds(0, 16)], nbm.at[1], nb_send.at[0], nb_recv.at[0], left, lane),
        3: rc(u_buf.at[0], nbu.at[1], nb_send.at[3], nb_recv.at[3], left, lane),
        5: rc(v_buf, nbv, nb_send.at[5], nb_recv.at[5], left, lane),
    }
    to_right = {
        1: rc(modes_ref.at[pl.ds(0, 16)], nbm.at[0], nb_send.at[1], nb_recv.at[1], right, lane),
        2: rc(t_buf.at[0, 1, lane], nbg, nb_send.at[2], nb_recv.at[2], right, lane),
        4: rc(u_buf.at[1], nbu.at[0], nb_send.at[4], nb_recv.at[4], right, lane),
    }

    def nb_start(which):
        copy, cond = (to_left[which], has_l) if which in to_left else (to_right[which], has_r)

        @pl.when(cond)
        def _():
            copy.start()

    def nb_wait(which):
        copy, cond = (to_left[which], has_r) if which in to_left else (to_right[which], has_l)

        @pl.when(cond)
        def _():
            copy.wait_recv()

    sends = []

    def ag_copy(r, f, src, slot, dst):
        piece = t_buf.at[r, f, src]
        return rc(piece, piece, ag_send.at[r, f, slot], ag_recv.at[r, f, src], s, dst)

    def ag_start(r, f):
        for d in range(1, X):
            copy = ag_copy(r, f, lane, d, lax.rem(x + d, X) * 2 + core)
            copy.start()
            sends.append(copy)
        copy = ag_copy(r, f, lane, 0, mate)
        copy.start()
        sends.append(copy)

    def ag_forward(r, f):
        for d in range(1, X):
            src = lax.rem(x + d, X) * 2 + core
            copy = ag_copy(r, f, src, X - 1 + d, mate)
            copy.wait_recv()
            copy.start()
            sends.append(copy)

    def lane_send(r, rows):
        for d in range(1, L):
            block = part.at[r, lane, pl.ds(0, rows)]
            copy = rc(block, block, ln_send.at[r, d], ln_recv.at[r, lane], s, lax.rem(lane + d, L))
            copy.start()
            sends.append(copy)

    def lane_sum(r, rows):
        total = part[r, lane, 0:rows]
        for d in range(1, L):
            src = lax.rem(lane + d, L)
            block = part.at[r, src, pl.ds(0, rows)]
            rc(block, block, ln_send.at[r, d], ln_recv.at[r, src], s, src).wait_recv()
            total = total + part[r, src, 0:rows]
        return total

    def sub_send(r, rows, value):
        red[r, s, 0:rows] = value
        block = red.at[r, s, pl.ds(0, rows)]
        for d in range(1, S):
            copy = rc(block, block, sb_send.at[r, d], sb_recv.at[r, s], lax.rem(s + d, S), lane)
            copy.start()
            sends.append(copy)

    def sub_wait(r, rows):
        for d in range(1, S):
            src = lax.rem(s + d, S)
            block = red.at[r, src, pl.ds(0, rows)]
            rc(block, block, sb_send.at[r, d], sb_recv.at[r, src], src, lane).wait_recv()

    def rhs_of(r):
        rows = []
        for t in range(S):
            row = red[r, t, 8:16]
            if t > 0:
                row = row + red[r, t - 1, 16:24]
            if t < S - 1:
                row = row + red[r, t + 1, 0:8]
            rows.append(row)
        return jnp.concatenate(rows, 0)

    def inner_of(r):
        total = red[r, 0, 24:25]
        for t in range(1, S):
            total = total + red[r, t, 24:25]
        return total

    def weights_of(r, inverse):
        wbuf[r, 0:8] = jnp.zeros((8, 128), f32)
        wbuf[r, n + 8:n + 16] = jnp.zeros((8, 128), f32)
        wbuf[r, 8:n + 8] = dot_nn(inverse, rhs_of(r))
        return wbuf[r, pl.ds(pl.multiple_of(s * 8, 8), 24)]

    nb_start(0)
    nb_start(1)
    ag_start(0, 1)
    nb_start(2)
    nb_wait(0)
    nb_wait(1)
    modes_left, modes_right = modes_ref[0:8], modes_ref[8:16]
    zero = jnp.zeros((8, R), f32)
    mt_l = jnp.concatenate([-nbm[0, 8:16], modes_left * m_l, zero], 0)
    mt_r = jnp.concatenate([zero, modes_right, -nbm[1, 0:8]], 0)
    mt[lane, 0] = mt_l
    mt[lane, 1] = mt_r
    gram = dot_nt(mt_l[8:16], mt_l) + dot_nt(mt_r[8:16], mt_r)
    part[0, lane, 0:24] = rows_times(mt_r, t_buf[0, 1, lane])
    part[0, lane, 24:32] = jnp.concatenate([gram, jnp.zeros((8, 104), f32)], 1)
    lane_send(0, 32)
    for d in range(1, L):
        copy = rc(mt.at[lane], mt.at[lane], mt_send.at[d], mt_recv.at[lane], s, lax.rem(lane + d, L))
        copy.start()
        sends.append(copy)
    nb_wait(2)
    t_buf[0, 0, lane] = -nbg[...]
    ag_start(0, 0)
    total = lane_sum(0, 32)
    idle = jnp.where(
        lax.broadcasted_iota(jnp.int32, (8, 128), 0) + 8 == lax.broadcasted_iota(jnp.int32, (8, 128), 1),
        modes_ref[16:24, 0:128], 0.0)
    sub_send(0, 32, jnp.concatenate([total[0:24], total[24:32] + idle], 0))
    ag_forward(0, 1)
    for d in range(1, L):
        src = lax.rem(lane + d, L)
        rc(mt.at[src], mt.at[src], mt_send.at[d], mt_recv.at[src], s, src).wait_recv()
    for j in range(L):
        for f in range(2):
            hi, mid, lo = thirds(mt[j, f])
            mt_t[j, f] = jnp.transpose(jnp.concatenate([hi, hi, mid, hi, mid, lo], 0)).astype(jnp.bfloat16)
    sub_wait(0, 32)

    rows = []
    for t in range(S):
        row = red[0, t, 24:32]
        if nw > 128:
            row = jnp.concatenate([row, jnp.zeros((8, nw - 128), f32)], 1)
        rows.append(pltpu.roll(row, (8 * (t - 1)) % nw, 1) if t != 1 else row)
    coarse = jnp.concatenate(rows, 0)
    row_at = lax.broadcasted_iota(jnp.int32, (n, nw), 0)
    col_at = lax.broadcasted_iota(jnp.int32, (n, nw), 1)

    def sweep(a, k, row, col):
        col = jnp.broadcast_to(col, (n, nw))
        scale = 1.0 / jnp.sum(jnp.where(row_at == k, col, 0.0), axis=0, keepdims=True) if n > 64 else 1.0 / col[k:k + 1]
        here = col_at == k
        scaled = jnp.where(here[0:1], -scale, row * scale)
        return jnp.where(row_at == k, scaled, jnp.where(here, 0.0, a) - col * scaled)

    if n <= 64:
        for t in range(S):
            for m in range(6):
                k = 8 * t + m
                coarse = sweep(coarse, k, coarse[k:k + 1], coarse[:, k:k + 1])
    else:
        def step(i, a):
            k = 8 * (i // 6) + lax.rem(i, 6)
            return sweep(a, k, jnp.sum(jnp.where(row_at == k, a, 0.0), axis=0, keepdims=True),
                         jnp.sum(jnp.where(col_at == k, a, 0.0), axis=1, keepdims=True))
        coarse = lax.fori_loop(0, 6 * S, step, coarse)
    pad = lax.rem(row_at, 8) >= 6
    inverse = jnp.where(pad, jnp.where(row_at == col_at, 1.0, 0.0), -coarse)[:, 0:n]

    ag_forward(0, 0)

    def multiply(r, matrix, weights):
        hi, mid, lo = thirds(weights)
        stacked = jnp.concatenate([hi, mid, hi, lo, mid, hi], 0).astype(jnp.bfloat16)
        order = [(lane, False), (mate, True)]
        order += [(lax.rem(x + d, X) * 2 + core, False) for d in range(1, X)]
        order += [(lax.rem(x + d, X) * 2 + 1 - core, True) for d in range(1, X)]
        for at, (j, wait) in enumerate(order):
            faces, his, los = [], [], []
            for f in (1, 0):
                if wait:
                    ag_copy(r, f, j, 0, mate).wait_recv()
                piece = t_buf[r, f, j] - jnp.dot(mt_t[j, f], stacked, preferred_element_type=f32)
                if at == 0:
                    own[r, f] = piece
                faces.append(jnp.concatenate(split(piece), 1))
                columns = pl.ds(pl.multiple_of(f * (L * R) + j * R, R), R)
                m_hi, m_lo = split(matrix[:, :, columns].reshape(2 * R, R))
                his.append(m_hi)
                los.append(m_lo)
            wide = jnp.dot(jnp.concatenate(his + los, 1), jnp.concatenate(faces + faces, 0),
                           preferred_element_type=f32)
            if at == 0:
                acc2[...] = wide
            else:
                acc2[...] += wide
        acc[0] = acc2[0:R, 0:128] + acc2[0:R, 128:256]
        acc[1] = acc2[R:2 * R, 0:128] + acc2[R:2 * R, 128:256]

    weights = weights_of(0, inverse)
    loads[0].wait()
    multiply(0, k_v, weights)

    u_buf[0] = acc[0] * 0.25
    u_buf[1] = acc[1] * 0.25
    nb_start(3)
    nb_start(4)
    dots = jnp.sum(own[0, 0] * u_buf[0] + own[0, 1] * u_buf[1], axis=0, keepdims=True)
    part[1, lane, 0:24] = rows_times(mt_l, u_buf[0]) + rows_times(mt_r, u_buf[1])
    part[1, lane, 24:32] = jnp.broadcast_to(dots, (8, 128))
    lane_send(1, 32)
    nb_wait(3)
    t_buf[1, 1, lane] = (u_buf[1] - nbu[1]) * m_r
    ag_start(1, 1)
    nb_wait(4)
    t_buf[1, 0, lane] = (u_buf[0] - nbu[0]) * m_l
    ag_start(1, 0)
    sub_send(1, 32, lane_sum(1, 32))
    ag_forward(1, 1)
    ag_forward(1, 0)
    sub_wait(1, 32)
    weights = weights_of(1, inverse)
    loads[1].wait()
    multiply(1, f_v, weights)

    v_buf[...] = acc[0]
    nb_start(5)
    dots = jnp.sum(own[1, 0] * acc[0] + own[1, 1] * acc[1], axis=0, keepdims=True)
    part[2, lane, 0:24] = rows_times(mt_l, acc[0]) + rows_times(mt_r, acc[1])
    part[2, lane, 24:32] = jnp.broadcast_to(dots, (8, 128))
    lane_send(2, 32)
    sub_send(2, 32, lane_sum(2, 32))
    nb_wait(5)
    image = (acc[1] - nbv[...]) * m_r
    sub_wait(2, 32)
    step_size = inner_of(1) / inner_of(2)
    image = image - dot_tn(mt_r, weights_of(2, inverse))
    mult_ref[...] = step_size * own[1, 1]
    res_ref[...] = own[0, 1] - step_size * image

    for copy in sends:
        copy.wait_send()

    @pl.when(has_l)
    def _():
        for copy in to_left.values():
            copy.wait_send()

    @pl.when(has_r)
    def _():
        for copy in to_right.values():
            copy.wait_send()


def per_device(gap, flexibility, stiffness, modes, mode_counts):
    S, L = lax.axis_size("sub"), lax.axis_size("ifc")
    R, n = gap.shape[1], 8 * lax.axis_size("sub")
    count, loads = modes.shape[1], gap.shape[2]
    live = (lax.axis_index("sub") < S - 1).astype(f32)
    active = (jnp.arange(8) < mode_counts[0]).astype(f32)
    faces = jnp.pad(jnp.swapaxes(modes[0], 0, 1), ((0, 0), (0, 8 - count), (0, 0)))
    faces = faces * active[None, :, None]
    idle = jnp.broadcast_to(1.0 - active[:, None], (8, R))
    packed = jnp.concatenate([faces[0], faces[1] * live, idle], 0)
    vm = pl.BlockSpec(memory_space=pltpu.VMEM)
    hbm = pl.BlockSpec(memory_space=pl.ANY)
    dma = pltpu.SemaphoreType.DMA
    mult, res = pl.pallas_call(
        functools.partial(kernel, S, L, R),
        out_shape=[jax.ShapeDtypeStruct((R, loads), f32)] * 2,
        in_specs=[vm, hbm, hbm, vm],
        out_specs=[vm, vm],
        scratch_shapes=[
            pltpu.VMEM((2, R, 2 * L * R), f32),
            pltpu.VMEM((2, R, 2 * L * R), f32),
            pltpu.VMEM((2, 16, R), f32),
            pltpu.VMEM((L, 2, 24, R), f32),
            pltpu.VMEM((2, 2, L, R, loads), f32),
            pltpu.VMEM((R, loads), f32),
            pltpu.VMEM((2, R, loads), f32),
            pltpu.VMEM((2, R, loads), f32),
            pltpu.VMEM((R, loads), f32),
            pltpu.VMEM((R, loads), f32),
            pltpu.VMEM((3, L, 32, 128), f32),
            pltpu.VMEM((3, S, 32, 128), f32),
            pltpu.VMEM((3, n + 16, 128), f32),
            pltpu.VMEM((2, 2, R, loads), f32),
            pltpu.VMEM((2, R, loads), f32),
            pltpu.VMEM((L, 2, R, 144), jnp.bfloat16),
            pltpu.VMEM((2 * R, 2 * loads), f32),
            dma((2,)),
            dma((6,)),
            dma((6,)),
            dma((2, 2, L)),
            dma((2, 2, L)),
            dma((L,)),
            dma((L,)),
            dma((3, L)),
            dma((3, L)),
            dma((3, S)),
            dma((3, S)),
        ],
        compiler_params=pltpu.CompilerParams(
            collective_id=0, has_side_effects=True, vmem_limit_bytes=60 * 1024 * 1024
        ),
    )(gap[0], stiffness[0], flexibility[0], packed)
    return (mult[None], res[None])


def solution(mesh):
    return jax.shard_map(
        per_device,
        mesh=mesh,
        in_specs=(
            P("sub", "ifc", None),
            P("sub", None, "ifc", None),
            P("sub", None, "ifc", None),
            P("sub", None, None, "ifc"),
            P("sub"),
        ),
        out_specs=(P("sub", "ifc", None), P("sub", "ifc", None)),
        check_vma=False,
    )
```

```python
import functools

import jax
import jax.numpy as jnp
from jax import lax
from jax.experimental import pallas as pl
from jax.experimental.pallas import tpu as pltpu
from jax.sharding import PartitionSpec as P

MESH = pl.DeviceIdType.MESH
precise = lax.Precision.HIGHEST
f32 = jnp.float32


def dot_nn(a, b):
    return lax.dot_general(a, b, (((1,), (0,)), ((), ())), precision=precise, preferred_element_type=f32)


def dot_nt(a, b):
    return lax.dot_general(a, b, (((1,), (1,)), ((), ())), precision=precise, preferred_element_type=f32)


def dot_tn(a, b):
    return lax.dot_general(a, b, (((0,), (0,)), ((), ())), precision=precise, preferred_element_type=f32)


def split(a):
    hi = a.astype(jnp.bfloat16)
    lo = (a - hi.astype(f32)).astype(jnp.bfloat16)
    return hi, lo


def thirds(a):
    hi = a.astype(jnp.bfloat16).astype(f32)
    mid = (a - hi).astype(jnp.bfloat16).astype(f32)
    lo = (a - hi - mid).astype(jnp.bfloat16).astype(f32)
    return hi, mid, lo


def rows_times(a, b):
    count, width = a.shape[0], b.shape[1]
    hi = a.astype(jnp.bfloat16).astype(f32)
    tall = jnp.concatenate([hi, a - hi], 0).astype(jnp.bfloat16)
    wide = jnp.dot(tall, jnp.concatenate(split(b), 1), preferred_element_type=f32)
    wide = wide[:count] + wide[count:]
    return wide[:, :width] + wide[:, width:]


def kernel(S, L, R, gap_ref, k_hbm, f_hbm, modes_ref, mult_ref, res_ref,
           k_v, f_v, nbm, mt, t_buf, nbg, u_buf, nbu, v_buf, nbv, part, red, wbuf, own, acc, mt_t, acc2,
           load_sem, nb_send, nb_recv, ag_send, ag_recv, mt_send, mt_recv,
           ln_send, ln_recv, sb_send, sb_recv):
    X = L // 2
    n = 8 * S
    nw = -(-n // 128) * 128
    s = lax.axis_index("sub")
    lane = lax.axis_index("ifc")
    x, core = lane // 2, lane % 2
    mate = x * 2 + (1 - core)
    has_l, has_r = s > 0, s < S - 1
    m_l, m_r = has_l.astype(f32), has_r.astype(f32)
    left, right = jnp.maximum(s - 1, 0), jnp.minimum(s + 1, S - 1)

    loads = [pltpu.make_async_copy(k_hbm, k_v, load_sem.at[0]),
             pltpu.make_async_copy(f_hbm, f_v, load_sem.at[1])]
    for load in loads:
        load.start()

    def rc(src, dst, ss, rs, sub, ln):
        return pltpu.make_async_remote_copy(src_ref=src, dst_ref=dst, send_sem=ss, recv_sem=rs,
                                            device_id=(sub, ln), device_id_type=MESH)

    barrier = pltpu.get_barrier_semaphore()
    for d in range(1, L):
        pl.semaphore_signal(barrier, inc=1, device_id=(s, lax.rem(lane + d, L)), device_id_type=MESH)
    for d in range(1, S):
        pl.semaphore_signal(barrier, inc=1, device_id=(lax.rem(s + d, S), lane), device_id_type=MESH)

    t_buf[0, 1, lane] = gap_ref[...] * m_r

    @pl.when(jnp.logical_not(has_l))
    def _():
        nbm[0] = jnp.zeros_like(nbm[0])
        nbg[...] = jnp.zeros_like(nbg)
        nbu[0] = jnp.zeros_like(nbu[0])

    @pl.when(jnp.logical_not(has_r))
    def _():
        nbm[1] = jnp.zeros_like(nbm[1])
        nbu[1] = jnp.zeros_like(nbu[1])
        nbv[...] = jnp.zeros_like(nbv)

    pl.semaphore_wait(barrier, (L - 1) + (S - 1))

    to_left = {
        0: rc(modes_ref.at[pl.ds(0, 16)], nbm.at[1], nb_send.at[0], nb_recv.at[0], left, lane),
        3: rc(u_buf.at[0], nbu.at[1], nb_send.at[3], nb_recv.at[3], left, lane),
        5: rc(v_buf, nbv, nb_send.at[5], nb_recv.at[5], left, lane),
    }
    to_right = {
        1: rc(modes_ref.at[pl.ds(0, 16)], nbm.at[0], nb_send.at[1], nb_recv.at[1], right, lane),
        2: rc(t_buf.at[0, 1, lane], nbg, nb_send.at[2], nb_recv.at[2], right, lane),
        4: rc(u_buf.at[1], nbu.at[0], nb_send.at[4], nb_recv.at[4], right, lane),
    }

    def nb_start(which):
        copy, cond = (to_left[which], has_l) if which in to_left else (to_right[which], has_r)

        @pl.when(cond)
        def _():
            copy.start()

    def nb_wait(which):
        copy, cond = (to_left[which], has_r) if which in to_left else (to_right[which], has_l)

        @pl.when(cond)
        def _():
            copy.wait_recv()

    sends = []

    def ag_copy(r, f, src, slot, dst):
        piece = t_buf.at[r, f, src]
        return rc(piece, piece, ag_send.at[r, f, slot], ag_recv.at[r, f, src], s, dst)

    def ag_start(r, f):
        for d in range(1, X):
            copy = ag_copy(r, f, lane, d, lax.rem(x + d, X) * 2 + core)
            copy.start()
            sends.append(copy)
        copy = ag_copy(r, f, lane, 0, mate)
        copy.start()
        sends.append(copy)

    def ag_forward(r, f):
        for d in range(1, X):
            src = lax.rem(x + d, X) * 2 + core
            copy = ag_copy(r, f, src, X - 1 + d, mate)
            copy.wait_recv()
            copy.start()
            sends.append(copy)

    def lane_send(r, rows):
        for d in range(1, L):
            block = part.at[r, lane, pl.ds(0, rows)]
            copy = rc(block, block, ln_send.at[r, d], ln_recv.at[r, lane], s, lax.rem(lane + d, L))
            copy.start()
            sends.append(copy)

    def lane_sum(r, rows):
        total = part[r, lane, 0:rows]
        for d in range(1, L):
            src = lax.rem(lane + d, L)
            block = part.at[r, src, pl.ds(0, rows)]
            rc(block, block, ln_send.at[r, d], ln_recv.at[r, src], s, src).wait_recv()
            total = total + part[r, src, 0:rows]
        return total

    def sub_send(r, rows, value):
        red[r, s, 0:rows] = value
        block = red.at[r, s, pl.ds(0, rows)]
        for d in range(1, S):
            copy = rc(block, block, sb_send.at[r, d], sb_recv.at[r, s], lax.rem(s + d, S), lane)
            copy.start()
            sends.append(copy)

    def sub_wait(r, rows):
        for d in range(1, S):
            src = lax.rem(s + d, S)
            block = red.at[r, src, pl.ds(0, rows)]
            rc(block, block, sb_send.at[r, d], sb_recv.at[r, src], src, lane).wait_recv()

    def rhs_of(r):
        rows = []
        for t in range(S):
            row = red[r, t, 8:16]
            if t > 0:
                row = row + red[r, t - 1, 16:24]
            if t < S - 1 and r > 0:
                row = row + red[r, t + 1, 0:8]
            rows.append(jnp.where(lax.broadcasted_iota(jnp.int32, (8, 128), 0) < 6, row, 0.0))
        return jnp.concatenate(rows, 0)

    def inner_of(r):
        total = red[r, 0, 14:15]
        for t in range(1, S):
            total = total + red[r, t, 14:15]
        return total

    def weights_of(r, inverse):
        wbuf[r, 0:8] = jnp.zeros((8, 128), f32)
        wbuf[r, n + 8:n + 16] = jnp.zeros((8, 128), f32)
        wbuf[r, 8:n + 8] = dot_nn(inverse, rhs_of(r))
        return wbuf[r, pl.ds(pl.multiple_of(s * 8, 8), 24)]

    nb_start(0)
    nb_start(1)
    ag_start(0, 1)
    nb_start(2)
    nb_wait(0)
    nb_wait(1)
    modes_left, modes_right = modes_ref[0:8], modes_ref[8:16]
    zero = jnp.zeros((8, R), f32)
    mt_l = jnp.concatenate([-nbm[0, 8:16], modes_left * m_l, zero], 0)
    mt_r = jnp.concatenate([zero, modes_right, -nbm[1, 0:8]], 0)
    mt[lane, 0] = mt_l
    mt[lane, 1] = mt_r
    gram = dot_nt(mt_l[8:16], mt_l) + dot_nt(mt_r[8:16], mt_r)
    part[0, lane, 8:24] = rows_times(mt_r, t_buf[0, 1, lane])[8:24]
    part[0, lane, 0:8] = jnp.concatenate([gram, jnp.zeros((8, 104), f32)], 1)
    lane_send(0, 24)
    for d in range(1, L):
        copy = rc(mt.at[lane], mt.at[lane], mt_send.at[d], mt_recv.at[lane], s, lax.rem(lane + d, L))
        copy.start()
        sends.append(copy)
    nb_wait(2)
    t_buf[0, 0, lane] = -nbg[...]
    ag_start(0, 0)
    total = lane_sum(0, 24)
    idle = jnp.where(
        lax.broadcasted_iota(jnp.int32, (8, 128), 0) + 8 == lax.broadcasted_iota(jnp.int32, (8, 128), 1),
        modes_ref[16:24, 0:128], 0.0)
    sub_send(0, 24, jnp.concatenate([total[0:8] + idle, total[8:24]], 0))
    ag_forward(0, 1)
    for d in range(1, L):
        src = lax.rem(lane + d, L)
        rc(mt.at[src], mt.at[src], mt_send.at[d], mt_recv.at[src], s, src).wait_recv()
    for j in range(L):
        for f in range(2):
            hi, mid, lo = thirds(mt[j, f])
            mt_t[j, f] = jnp.transpose(jnp.concatenate([hi, hi, mid, hi, mid, lo], 0)).astype(jnp.bfloat16)
    sub_wait(0, 24)

    rows = []
    for t in range(S):
        row = red[0, t, 0:8]
        if nw > 128:
            row = jnp.concatenate([row, jnp.zeros((8, nw - 128), f32)], 1)
        rows.append(pltpu.roll(row, (8 * (t - 1)) % nw, 1) if t != 1 else row)
    blocks = rows
    coarse = jnp.concatenate(rows, 0)
    row_at = lax.broadcasted_iota(jnp.int32, (n, nw), 0)
    col_at = lax.broadcasted_iota(jnp.int32, (n, nw), 1)

    def sweep(a, k, row, col):
        col = jnp.broadcast_to(col, (n, nw))
        scale = 1.0 / jnp.sum(jnp.where(row_at == k, col, 0.0), axis=0, keepdims=True) if n > 64 else 1.0 / col[k:k + 1]
        here = col_at == k
        scaled = jnp.where(here[0:1], -scale, row * scale)
        return jnp.where(row_at == k, scaled, jnp.where(here, 0.0, a) - col * scaled)

    if n <= 64:
        couples = [[abs(i - j) <= 1 for j in range(S)] for i in range(S)]
        row8, col8 = row_at[0:8], col_at[0:8]
        remaining = list(range(S))
        while remaining:
            chosen, remaining = remaining[0::2], remaining[1::2]
            for m in range(6):
                fresh = list(blocks)
                for t in chosen:
                    k = 8 * t + m
                    cols = {i: jnp.broadcast_to(blocks[i][:, k:k + 1], (8, nw)) for i in range(S) if couples[t][i]}
                    scale = 1.0 / cols[t][m:m + 1]
                    here = col8 == k
                    scaled = jnp.where(here[0:1], -scale, blocks[t][m:m + 1] * scale)
                    for i, col in cols.items():
                        fresh[i] = jnp.where(here, 0.0, fresh[i]) - col * scaled
                    fresh[t] = jnp.where(row8 == m, scaled, fresh[t])
                blocks = fresh
            for t in chosen:
                near = [i for i in range(S) if couples[t][i]]
                for i in near:
                    for j in near:
                        couples[i][j] = True
        coarse = jnp.concatenate(blocks, 0)
    else:
        def step(i, a):
            k = 8 * (i // 6) + lax.rem(i, 6)
            return sweep(a, k, jnp.sum(jnp.where(row_at == k, a, 0.0), axis=0, keepdims=True),
                         jnp.sum(jnp.where(col_at == k, a, 0.0), axis=1, keepdims=True))
        coarse = lax.fori_loop(0, 6 * S, step, coarse)
    pad = lax.rem(row_at, 8) >= 6
    inverse = jnp.where(pad, jnp.where(row_at == col_at, 1.0, 0.0), -coarse)[:, 0:n]

    ag_forward(0, 0)

    def multiply(r, matrix, weights):
        hi, mid, lo = thirds(weights)
        stacked = jnp.concatenate([hi, mid, hi, lo, mid, hi], 0).astype(jnp.bfloat16)
        order = [(lane, False), (mate, True)]
        order += [(lax.rem(x + d, X) * 2 + core, False) for d in range(1, X)]
        order += [(lax.rem(x + d, X) * 2 + 1 - core, True) for d in range(1, X)]
        for at, (j, wait) in enumerate(order):
            faces, his, los = [], [], []
            for f in (1, 0):
                if wait:
                    ag_copy(r, f, j, 0, mate).wait_recv()
                piece = t_buf[r, f, j] - jnp.dot(mt_t[j, f], stacked, preferred_element_type=f32)
                if at == 0:
                    own[r, f] = piece
                faces.append(jnp.concatenate(split(piece), 1))
                columns = pl.ds(pl.multiple_of(f * (L * R) + j * R, R), R)
                m_hi, m_lo = split(matrix[:, :, columns].reshape(2 * R, R))
                his.append(m_hi)
                los.append(m_lo)
            wide = jnp.dot(jnp.concatenate(his + los, 1), jnp.concatenate(faces + faces, 0),
                           preferred_element_type=f32)
            if at == 0:
                acc2[...] = wide
            else:
                acc2[...] += wide
        acc[0] = acc2[0:R, 0:128] + acc2[0:R, 128:256]
        acc[1] = acc2[R:2 * R, 0:128] + acc2[R:2 * R, 128:256]

    weights = weights_of(0, inverse)
    loads[0].wait()
    multiply(0, k_v, weights)

    u_buf[0] = acc[0] * 0.25
    u_buf[1] = acc[1] * 0.25
    nb_start(3)
    nb_start(4)
    dots = jnp.sum(own[0, 0] * u_buf[0] + own[0, 1] * u_buf[1], axis=0, keepdims=True)
    part[1, lane, 0:24] = rows_times(mt_l, u_buf[0]) + rows_times(mt_r, u_buf[1])
    part[1, lane, 14:15] = dots
    lane_send(1, 24)
    nb_wait(3)
    t_buf[1, 1, lane] = (u_buf[1] - nbu[1]) * m_r
    ag_start(1, 1)
    nb_wait(4)
    t_buf[1, 0, lane] = (u_buf[0] - nbu[0]) * m_l
    ag_start(1, 0)
    sub_send(1, 24, lane_sum(1, 24))
    ag_forward(1, 1)
    ag_forward(1, 0)
    sub_wait(1, 24)
    weights = weights_of(1, inverse)
    loads[1].wait()
    multiply(1, f_v, weights)

    v_buf[...] = acc[0]
    nb_start(5)
    dots = jnp.sum(own[1, 0] * acc[0] + own[1, 1] * acc[1], axis=0, keepdims=True)
    part[2, lane, 0:24] = rows_times(mt_l, acc[0]) + rows_times(mt_r, acc[1])
    part[2, lane, 14:15] = dots
    lane_send(2, 24)
    sub_send(2, 24, lane_sum(2, 24))
    nb_wait(5)
    image = (acc[1] - nbv[...]) * m_r
    sub_wait(2, 24)
    step_size = inner_of(1) / inner_of(2)
    image = image - dot_tn(mt_r, weights_of(2, inverse))
    mult_ref[...] = step_size * own[1, 1]
    res_ref[...] = own[0, 1] - step_size * image

    for copy in sends:
        copy.wait_send()

    @pl.when(has_l)
    def _():
        for copy in to_left.values():
            copy.wait_send()

    @pl.when(has_r)
    def _():
        for copy in to_right.values():
            copy.wait_send()


def per_device(gap, flexibility, stiffness, modes, mode_counts):
    S, L = lax.axis_size("sub"), lax.axis_size("ifc")
    R, n = gap.shape[1], 8 * lax.axis_size("sub")
    count, loads = modes.shape[1], gap.shape[2]
    live = (lax.axis_index("sub") < S - 1).astype(f32)
    active = (jnp.arange(8) < mode_counts[0]).astype(f32)
    faces = jnp.pad(jnp.swapaxes(modes[0], 0, 1), ((0, 0), (0, 8 - count), (0, 0)))
    faces = faces * active[None, :, None]
    idle = jnp.broadcast_to(1.0 - active[:, None], (8, R))
    packed = jnp.concatenate([faces[0], faces[1] * live, idle], 0)
    vm = pl.BlockSpec(memory_space=pltpu.VMEM)
    hbm = pl.BlockSpec(memory_space=pl.ANY)
    dma = pltpu.SemaphoreType.DMA
    mult, res = pl.pallas_call(
        functools.partial(kernel, S, L, R),
        out_shape=[jax.ShapeDtypeStruct((R, loads), f32)] * 2,
        in_specs=[vm, hbm, hbm, vm],
        out_specs=[vm, vm],
        scratch_shapes=[
            pltpu.VMEM((2, R, 2 * L * R), f32),
            pltpu.VMEM((2, R, 2 * L * R), f32),
            pltpu.VMEM((2, 16, R), f32),
            pltpu.VMEM((L, 2, 24, R), f32),
            pltpu.VMEM((2, 2, L, R, loads), f32),
            pltpu.VMEM((R, loads), f32),
            pltpu.VMEM((2, R, loads), f32),
            pltpu.VMEM((2, R, loads), f32),
            pltpu.VMEM((R, loads), f32),
            pltpu.VMEM((R, loads), f32),
            pltpu.VMEM((3, L, 24, 128), f32),
            pltpu.VMEM((3, S, 24, 128), f32),
            pltpu.VMEM((3, n + 16, 128), f32),
            pltpu.VMEM((2, 2, R, loads), f32),
            pltpu.VMEM((2, R, loads), f32),
            pltpu.VMEM((L, 2, R, 144), jnp.bfloat16),
            pltpu.VMEM((2 * R, 2 * loads), f32),
            dma((2,)),
            dma((6,)),
            dma((6,)),
            dma((2, 2, L)),
            dma((2, 2, L)),
            dma((L,)),
            dma((L,)),
            dma((3, L)),
            dma((3, L)),
            dma((3, S)),
            dma((3, S)),
        ],
        compiler_params=pltpu.CompilerParams(
            collective_id=0, has_side_effects=True, vmem_limit_bytes=60 * 1024 * 1024
        ),
    )(gap[0], stiffness[0], flexibility[0], packed)
    return (mult[None], res[None])


def solution(mesh):
    return jax.shard_map(
        per_device,
        mesh=mesh,
        in_specs=(
            P("sub", "ifc", None),
            P("sub", None, "ifc", None),
            P("sub", None, "ifc", None),
            P("sub", None, None, "ifc"),
            P("sub"),
        ),
        out_specs=(P("sub", "ifc", None), P("sub", "ifc", None)),
        check_vma=False,
    )
```

```python
import functools

import jax
import jax.numpy as jnp
from jax import lax
from jax.experimental import pallas as pl
from jax.experimental.pallas import tpu as pltpu
from jax.sharding import PartitionSpec as P

MESH = pl.DeviceIdType.MESH
precise = lax.Precision.HIGHEST
f32 = jnp.float32


def dot_nn(a, b):
    return lax.dot_general(a, b, (((1,), (0,)), ((), ())), precision=precise, preferred_element_type=f32)


def dot_nt(a, b):
    return lax.dot_general(a, b, (((1,), (1,)), ((), ())), precision=precise, preferred_element_type=f32)


def dot_tn(a, b):
    return lax.dot_general(a, b, (((0,), (0,)), ((), ())), precision=precise, preferred_element_type=f32)


def split(a):
    hi = a.astype(jnp.bfloat16)
    lo = (a - hi.astype(f32)).astype(jnp.bfloat16)
    return hi, lo


def thirds(a):
    hi = a.astype(jnp.bfloat16).astype(f32)
    mid = (a - hi).astype(jnp.bfloat16).astype(f32)
    lo = (a - hi - mid).astype(jnp.bfloat16).astype(f32)
    return hi, mid, lo


def rows_times(a, b):
    count, width = a.shape[0], b.shape[1]
    hi = a.astype(jnp.bfloat16).astype(f32)
    tall = jnp.concatenate([hi, a - hi], 0).astype(jnp.bfloat16)
    wide = jnp.dot(tall, jnp.concatenate(split(b), 1), preferred_element_type=f32)
    wide = wide[:count] + wide[count:]
    return wide[:, :width] + wide[:, width:]


def kernel(S, L, R, gap_ref, k_hbm, f_hbm, modes_ref, mult_ref, res_ref,
           k_v, f_v, nbm, mt, t_buf, nbg, u_buf, nbu, v_buf, nbv, part, red, wbuf, own, acc, mt_t, acc2,
           load_sem, nb_send, nb_recv, ag_send, ag_recv, mt_send, mt_recv,
           ln_send, ln_recv, sb_send, sb_recv):
    X = L // 2
    n = 8 * S
    nw = -(-n // 128) * 128
    s = lax.axis_index("sub")
    lane = lax.axis_index("ifc")
    x, core = lane // 2, lane % 2
    mate = x * 2 + (1 - core)
    has_l, has_r = s > 0, s < S - 1
    m_l, m_r = has_l.astype(f32), has_r.astype(f32)
    left, right = jnp.maximum(s - 1, 0), jnp.minimum(s + 1, S - 1)

    loads = [pltpu.make_async_copy(k_hbm, k_v, load_sem.at[0]),
             pltpu.make_async_copy(f_hbm, f_v, load_sem.at[1])]
    for load in loads:
        load.start()

    def rc(src, dst, ss, rs, sub, ln):
        return pltpu.make_async_remote_copy(src_ref=src, dst_ref=dst, send_sem=ss, recv_sem=rs,
                                            device_id=(sub, ln), device_id_type=MESH)

    barrier = pltpu.get_barrier_semaphore()
    for d in range(1, L):
        pl.semaphore_signal(barrier, inc=1, device_id=(s, lax.rem(lane + d, L)), device_id_type=MESH)
    for d in range(1, S):
        pl.semaphore_signal(barrier, inc=1, device_id=(lax.rem(s + d, S), lane), device_id_type=MESH)

    t_buf[0, 1, lane] = gap_ref[...] * m_r

    @pl.when(jnp.logical_not(has_l))
    def _():
        nbm[0] = jnp.zeros_like(nbm[0])
        nbg[...] = jnp.zeros_like(nbg)
        nbu[0] = jnp.zeros_like(nbu[0])

    @pl.when(jnp.logical_not(has_r))
    def _():
        nbm[1] = jnp.zeros_like(nbm[1])
        nbu[1] = jnp.zeros_like(nbu[1])
        nbv[...] = jnp.zeros_like(nbv)

    pl.semaphore_wait(barrier, (L - 1) + (S - 1))

    to_left = {
        0: rc(modes_ref.at[pl.ds(0, 16)], nbm.at[1], nb_send.at[0], nb_recv.at[0], left, lane),
        3: rc(u_buf.at[0], nbu.at[1], nb_send.at[3], nb_recv.at[3], left, lane),
        5: rc(v_buf, nbv, nb_send.at[5], nb_recv.at[5], left, lane),
    }
    to_right = {
        1: rc(modes_ref.at[pl.ds(0, 16)], nbm.at[0], nb_send.at[1], nb_recv.at[1], right, lane),
        2: rc(t_buf.at[0, 1, lane], nbg, nb_send.at[2], nb_recv.at[2], right, lane),
        4: rc(u_buf.at[1], nbu.at[0], nb_send.at[4], nb_recv.at[4], right, lane),
    }

    def nb_start(which):
        copy, cond = (to_left[which], has_l) if which in to_left else (to_right[which], has_r)

        @pl.when(cond)
        def _():
            copy.start()

    def nb_wait(which):
        copy, cond = (to_left[which], has_r) if which in to_left else (to_right[which], has_l)

        @pl.when(cond)
        def _():
            copy.wait_recv()

    sends = []

    def ag_copy(r, f, src, slot, dst):
        piece = t_buf.at[r, f, src]
        return rc(piece, piece, ag_send.at[r, f, slot], ag_recv.at[r, f, src], s, dst)

    def ag_start(r, f):
        for d in range(1, X):
            copy = ag_copy(r, f, lane, d, lax.rem(x + d, X) * 2 + core)
            copy.start()
            sends.append(copy)
        copy = ag_copy(r, f, lane, 0, mate)
        copy.start()
        sends.append(copy)

    def ag_forward(r, f):
        for d in range(1, X):
            src = lax.rem(x + d, X) * 2 + core
            copy = ag_copy(r, f, src, X - 1 + d, mate)
            copy.wait_recv()
            copy.start()
            sends.append(copy)

    def lane_send(r, rows):
        for d in range(1, L):
            block = part.at[r, lane, pl.ds(0, rows)]
            copy = rc(block, block, ln_send.at[r, d], ln_recv.at[r, lane], s, lax.rem(lane + d, L))
            copy.start()
            sends.append(copy)

    def lane_sum(r, rows):
        total = part[r, lane, 0:rows]
        for d in range(1, L):
            src = lax.rem(lane + d, L)
            block = part.at[r, src, pl.ds(0, rows)]
            rc(block, block, ln_send.at[r, d], ln_recv.at[r, src], s, src).wait_recv()
            total = total + part[r, src, 0:rows]
        return total

    def sub_send(r, rows, value):
        red[r, s, 0:rows] = value
        block = red.at[r, s, pl.ds(0, rows)]
        for d in range(1, S):
            copy = rc(block, block, sb_send.at[r, d], sb_recv.at[r, s], lax.rem(s + d, S), lane)
            copy.start()
            sends.append(copy)

    def sub_wait(r, rows):
        for d in range(1, S):
            src = lax.rem(s + d, S)
            block = red.at[r, src, pl.ds(0, rows)]
            rc(block, block, sb_send.at[r, d], sb_recv.at[r, src], src, lane).wait_recv()

    def rhs_of(r):
        rows = []
        for t in range(S):
            row = red[r, t, 8:16]
            if t > 0:
                row = row + red[r, t - 1, 16:24]
            if t < S - 1 and r > 0:
                row = row + red[r, t + 1, 0:8]
            rows.append(jnp.where(lax.broadcasted_iota(jnp.int32, (8, 128), 0) < 6, row, 0.0))
        return jnp.concatenate(rows, 0)

    def inner_of(r):
        total = red[r, 0, 14:15]
        for t in range(1, S):
            total = total + red[r, t, 14:15]
        return total

    def weights_of(r, inverse):
        wbuf[r, 0:8] = jnp.zeros((8, 128), f32)
        wbuf[r, n + 8:n + 16] = jnp.zeros((8, 128), f32)
        wbuf[r, 8:n + 8] = dot_nn(inverse, rhs_of(r))
        return wbuf[r, pl.ds(pl.multiple_of(s * 8, 8), 24)]

    nb_start(0)
    nb_start(1)
    nb_start(2)
    nb_wait(0)
    nb_wait(1)
    modes_left, modes_right = modes_ref[0:8], modes_ref[8:16]
    zero = jnp.zeros((8, R), f32)
    mt_l = jnp.concatenate([-nbm[0, 8:16], modes_left * m_l, zero], 0)
    mt_r = jnp.concatenate([zero, modes_right, -nbm[1, 0:8]], 0)
    mt[lane, 0] = mt_l
    mt[lane, 1] = mt_r
    gram = dot_nt(mt_l[8:16], mt_l) + dot_nt(mt_r[8:16], mt_r)
    part[0, lane, 8:24] = rows_times(mt_r, t_buf[0, 1, lane])[8:24]
    part[0, lane, 0:8] = jnp.concatenate([gram, jnp.zeros((8, 104), f32)], 1)
    lane_send(0, 24)
    for d in range(1, L):
        copy = rc(mt.at[lane], mt.at[lane], mt_send.at[d], mt_recv.at[lane], s, lax.rem(lane + d, L))
        copy.start()
        sends.append(copy)
    ag_start(0, 1)
    nb_wait(2)
    t_buf[0, 0, lane] = -nbg[...]
    ag_start(0, 0)
    total = lane_sum(0, 24)
    idle = jnp.where(
        lax.broadcasted_iota(jnp.int32, (8, 128), 0) + 8 == lax.broadcasted_iota(jnp.int32, (8, 128), 1),
        modes_ref[16:24, 0:128], 0.0)
    sub_send(0, 24, jnp.concatenate([total[0:8] + idle, total[8:24]], 0))
    ag_forward(0, 1)
    for d in range(1, L):
        src = lax.rem(lane + d, L)
        rc(mt.at[src], mt.at[src], mt_send.at[d], mt_recv.at[src], s, src).wait_recv()
    for j in range(L):
        for f in range(2):
            hi, mid, lo = thirds(mt[j, f])
            mt_t[j, f] = jnp.transpose(jnp.concatenate([hi, hi, mid, hi, mid, lo], 0)).astype(jnp.bfloat16)
    sub_wait(0, 24)

    rows = []
    for t in range(S):
        row = red[0, t, 0:8]
        if nw > 128:
            row = jnp.concatenate([row, jnp.zeros((8, nw - 128), f32)], 1)
        rows.append(pltpu.roll(row, (8 * (t - 1)) % nw, 1) if t != 1 else row)
    blocks = rows
    coarse = jnp.concatenate(rows, 0)
    row_at = lax.broadcasted_iota(jnp.int32, (n, nw), 0)
    col_at = lax.broadcasted_iota(jnp.int32, (n, nw), 1)

    def sweep(a, k, row, col):
        col = jnp.broadcast_to(col, (n, nw))
        scale = 1.0 / jnp.sum(jnp.where(row_at == k, col, 0.0), axis=0, keepdims=True) if n > 64 else 1.0 / col[k:k + 1]
        here = col_at == k
        scaled = jnp.where(here[0:1], -scale, row * scale)
        return jnp.where(row_at == k, scaled, jnp.where(here, 0.0, a) - col * scaled)

    if n <= 64:
        couples = [[abs(i - j) <= 1 for j in range(S)] for i in range(S)]
        row8, col8 = row_at[0:8], col_at[0:8]
        remaining = list(range(S))
        while remaining:
            chosen, remaining = remaining[0::2], remaining[1::2]
            for m in range(6):
                fresh = list(blocks)
                for t in chosen:
                    k = 8 * t + m
                    cols = {i: jnp.broadcast_to(blocks[i][:, k:k + 1], (8, nw)) for i in range(S) if couples[t][i]}
                    scale = 1.0 / cols[t][m:m + 1]
                    here = col8 == k
                    scaled = jnp.where(here[0:1], -scale, blocks[t][m:m + 1] * scale)
                    for i, col in cols.items():
                        fresh[i] = jnp.where(here, 0.0, fresh[i]) - col * scaled
                    fresh[t] = jnp.where(row8 == m, scaled, fresh[t])
                blocks = fresh
            for t in chosen:
                near = [i for i in range(S) if couples[t][i]]
                for i in near:
                    for j in near:
                        couples[i][j] = True
        coarse = jnp.concatenate(blocks, 0)
    else:
        def step(i, a):
            k = 8 * (i // 6) + lax.rem(i, 6)
            return sweep(a, k, jnp.sum(jnp.where(row_at == k, a, 0.0), axis=0, keepdims=True),
                         jnp.sum(jnp.where(col_at == k, a, 0.0), axis=1, keepdims=True))
        coarse = lax.fori_loop(0, 6 * S, step, coarse)
    pad = lax.rem(row_at, 8) >= 6
    inverse = jnp.where(pad, jnp.where(row_at == col_at, 1.0, 0.0), -coarse)[:, 0:n]

    ag_forward(0, 0)

    def multiply(r, matrix, weights):
        hi, mid, lo = thirds(weights)
        stacked = jnp.concatenate([hi, mid, hi, lo, mid, hi], 0).astype(jnp.bfloat16)
        order = [(lane, False), (mate, True)]
        order += [(lax.rem(x + d, X) * 2 + core, False) for d in range(1, X)]
        order += [(lax.rem(x + d, X) * 2 + 1 - core, True) for d in range(1, X)]
        for at, (j, wait) in enumerate(order):
            faces, his, los = [], [], []
            for f in (1, 0):
                if wait:
                    ag_copy(r, f, j, 0, mate).wait_recv()
                piece = t_buf[r, f, j] - jnp.dot(mt_t[j, f], stacked, preferred_element_type=f32)
                if at == 0:
                    own[r, f] = piece
                faces.append(jnp.concatenate(split(piece), 1))
                columns = pl.ds(pl.multiple_of(f * (L * R) + j * R, R), R)
                m_hi, m_lo = split(matrix[:, :, columns].reshape(2 * R, R))
                his.append(m_hi)
                los.append(m_lo)
            wide = jnp.dot(jnp.concatenate(his + los, 1), jnp.concatenate(faces + faces, 0),
                           preferred_element_type=f32)
            if at == 0:
                acc2[...] = wide
            else:
                acc2[...] += wide
        acc[0] = acc2[0:R, 0:128] + acc2[0:R, 128:256]
        acc[1] = acc2[R:2 * R, 0:128] + acc2[R:2 * R, 128:256]

    weights = weights_of(0, inverse)
    loads[0].wait()
    multiply(0, k_v, weights)

    u_buf[0] = acc[0] * 0.25
    u_buf[1] = acc[1] * 0.25
    nb_start(3)
    nb_start(4)
    dots = jnp.sum(own[0, 0] * u_buf[0] + own[0, 1] * u_buf[1], axis=0, keepdims=True)
    part[1, lane, 0:24] = rows_times(mt_l, u_buf[0]) + rows_times(mt_r, u_buf[1])
    part[1, lane, 14:15] = dots
    lane_send(1, 24)
    nb_wait(3)
    t_buf[1, 1, lane] = (u_buf[1] - nbu[1]) * m_r
    ag_start(1, 1)
    nb_wait(4)
    t_buf[1, 0, lane] = (u_buf[0] - nbu[0]) * m_l
    ag_start(1, 0)
    sub_send(1, 24, lane_sum(1, 24))
    ag_forward(1, 1)
    ag_forward(1, 0)
    sub_wait(1, 24)
    weights = weights_of(1, inverse)
    loads[1].wait()
    multiply(1, f_v, weights)

    v_buf[...] = acc[0]
    nb_start(5)
    dots = jnp.sum(own[1, 0] * acc[0] + own[1, 1] * acc[1], axis=0, keepdims=True)
    part[2, lane, 0:24] = rows_times(mt_l, acc[0]) + rows_times(mt_r, acc[1])
    part[2, lane, 14:15] = dots
    lane_send(2, 24)
    sub_send(2, 24, lane_sum(2, 24))
    nb_wait(5)
    image = (acc[1] - nbv[...]) * m_r
    sub_wait(2, 24)
    step_size = inner_of(1) / inner_of(2)
    image = image - dot_tn(mt_r, weights_of(2, inverse))
    mult_ref[...] = step_size * own[1, 1]
    res_ref[...] = own[0, 1] - step_size * image

    for copy in sends:
        copy.wait_send()

    @pl.when(has_l)
    def _():
        for copy in to_left.values():
            copy.wait_send()

    @pl.when(has_r)
    def _():
        for copy in to_right.values():
            copy.wait_send()


def per_device(gap, flexibility, stiffness, modes, mode_counts):
    S, L = lax.axis_size("sub"), lax.axis_size("ifc")
    R, n = gap.shape[1], 8 * lax.axis_size("sub")
    count, loads = modes.shape[1], gap.shape[2]
    live = (lax.axis_index("sub") < S - 1).astype(f32)
    active = (jnp.arange(8) < mode_counts[0]).astype(f32)
    faces = jnp.pad(jnp.swapaxes(modes[0], 0, 1), ((0, 0), (0, 8 - count), (0, 0)))
    faces = faces * active[None, :, None]
    idle = jnp.broadcast_to(1.0 - active[:, None], (8, R))
    packed = jnp.concatenate([faces[0], faces[1] * live, idle], 0)
    vm = pl.BlockSpec(memory_space=pltpu.VMEM)
    hbm = pl.BlockSpec(memory_space=pl.ANY)
    dma = pltpu.SemaphoreType.DMA
    mult, res = pl.pallas_call(
        functools.partial(kernel, S, L, R),
        out_shape=[jax.ShapeDtypeStruct((R, loads), f32)] * 2,
        in_specs=[vm, hbm, hbm, vm],
        out_specs=[vm, vm],
        scratch_shapes=[
            pltpu.VMEM((2, R, 2 * L * R), f32),
            pltpu.VMEM((2, R, 2 * L * R), f32),
            pltpu.VMEM((2, 16, R), f32),
            pltpu.VMEM((L, 2, 24, R), f32),
            pltpu.VMEM((2, 2, L, R, loads), f32),
            pltpu.VMEM((R, loads), f32),
            pltpu.VMEM((2, R, loads), f32),
            pltpu.VMEM((2, R, loads), f32),
            pltpu.VMEM((R, loads), f32),
            pltpu.VMEM((R, loads), f32),
            pltpu.VMEM((3, L, 24, 128), f32),
            pltpu.VMEM((3, S, 24, 128), f32),
            pltpu.VMEM((3, n + 16, 128), f32),
            pltpu.VMEM((2, 2, R, loads), f32),
            pltpu.VMEM((2, R, loads), f32),
            pltpu.VMEM((L, 2, R, 144), jnp.bfloat16),
            pltpu.VMEM((2 * R, 2 * loads), f32),
            dma((2,)),
            dma((6,)),
            dma((6,)),
            dma((2, 2, L)),
            dma((2, 2, L)),
            dma((L,)),
            dma((L,)),
            dma((3, L)),
            dma((3, L)),
            dma((3, S)),
            dma((3, S)),
        ],
        compiler_params=pltpu.CompilerParams(
            collective_id=0, has_side_effects=True, vmem_limit_bytes=52 * 1024 * 1024
        ),
    )(gap[0], stiffness[0], flexibility[0], packed)
    return (mult[None], res[None])


def solution(mesh):
    return jax.shard_map(
        per_device,
        mesh=mesh,
        in_specs=(
            P("sub", "ifc", None),
            P("sub", None, "ifc", None),
            P("sub", None, "ifc", None),
            P("sub", None, None, "ifc"),
            P("sub"),
        ),
        out_specs=(P("sub", "ifc", None), P("sub", "ifc", None)),
        check_vma=False,
    )
```
